32 devices in a mesh: groups: 2 (over y), row: 8 (over z, x), col: 2 (over core).
Axes of the slice: x: 2, y: 2, z: 4, core: 2. Of those that a mesh axis runs over, the one named last changes fastest.
Arguments:
- acts: bfloat16 [2048, 8192], P(('groups', 'row'), 'col'), parts along dimension 0, may hold values from -6 to 6
- w_value: bfloat16 [8192, 1024], P('row', 'col'), may hold values from -0.0625 to 0.0625
- adapt_down: bfloat16 [8192, 64], P('row'), may hold values from -0.0625 to 0.0625
- adapter_up_factor: bfloat16 [64, 1024], P(None, 'col'), may hold values from -0.375 to 0.375
- cotangent: bfloat16 [2048, 1024], P(('groups', 'row'), 'col'), parts along dimension 0, may hold values from -6 to 6
Outputs:
- values: bfloat16 [2048, 1024], P(('groups', 'row'), 'col'), parts along dimension 0
- grad_acts: bfloat16 [2048, 8192], P(('groups', 'row'), 'col'), parts along dimension 0
- grad_down: float32 [16384, 64], P(('groups', 'row', 'col')), parts along dimension 0
- up_factor_gradient: float32 [128, 1024], P('groups', 'col'), parts along dimension 0
The draws below stay inside these ranges and needn't reach their ends.
There are 2 independent parts, one for each index of `groups`. The reference program is written for one: setup_inputs(seed, part) draws one part's arguments, and reference() takes and returns one part's arrays. A program takes and returns all parts, laid end to end along the dimension named above; an argument that names none is the same for every part. Nothing has to cross between parts.
All inputs are finite; a program needn't handle non-finite values.
Results may differ from the reference program's by a relative error of at most 0.01.
Values may be sent and summed in bfloat16 or wider, within the bound.
A program may use at most 64 MiB of HBM per device.

```python
import math
import jax
import jax.numpy as jnp
from jax import lax

D = 8192
KV = 1024
R = 64
TOKENS = 1024
N_COL = 2


def steps_of(own_key, dims, split, low, high):
    loudness, own = 1.0, jax.random.fold_in(own_key, 6)
    for axis_at, parts in split:
        steps = jnp.exp(jax.random.uniform(jax.random.fold_in(own, axis_at), (parts,), jnp.float32, low / len(split), high / len(split)))
        loudness = loudness * jnp.repeat(steps, dims[axis_at] // parts).reshape([-1 if axis == axis_at else 1 for axis in range(len(dims))])
    return loudness


def centred(rng, extent, scale, limit, cuts=(), dtype=jnp.bfloat16):
    entries = scale * jax.random.normal(rng, extent, jnp.float32)
    if cuts:
        entries = entries * steps_of(rng, extent, cuts, -0.22, 0.18)
    return jnp.clip(entries, -limit, limit).astype(dtype)


def setup_inputs(seed: int = 0, part: int = 0) -> dict:
    arg_keys = jax.random.split(jax.random.key(seed), 6)
    own_keys = jax.random.split(jax.random.fold_in(arg_keys[5], part), 6)
    acts = centred(own_keys[0], (TOKENS, D), 1.0, 6.0, ((0, 8), (1, 2)))
    w_value = centred(arg_keys[1], (D, KV), D ** -0.5, 0.0625, ((0, 8), (1, 2)))
    adapt_down = centred(arg_keys[2], (D, R), D ** -0.5, 0.0625, ((0, 8),))
    adapter_up_factor = centred(arg_keys[3], (R, KV), (4 * R) ** -0.5, 0.375, ((1, 2),))
    cotangent = centred(own_keys[4], (TOKENS, KV), 1.0, 6.0, ((0, 8), (1, 2)))
    return {"acts": acts, "w_value": w_value, "adapt_down": adapt_down, "adapter_up_factor": adapter_up_factor, "cotangent": cotangent}


ADAPTER_SCALE = 2.0

def reference(acts, w_value, adapt_down, adapter_up_factor, cotangent):
    low_rank_input = jnp.dot(acts, adapt_down, preferred_element_type=jnp.float32).astype(jnp.bfloat16)
    base_output = jnp.dot(acts, w_value, preferred_element_type=jnp.float32)
    adapter_output = jnp.dot(low_rank_input, adapter_up_factor, preferred_element_type=jnp.float32)
    values = (base_output + ADAPTER_SCALE * adapter_output).astype(jnp.bfloat16)
    backward_result = (ADAPTER_SCALE * jnp.dot(cotangent, adapter_up_factor.T, preferred_element_type=jnp.float32)).astype(jnp.bfloat16)
    gradient_norm = 1.0 / math.sqrt(TOKENS)
    up_factor_gradient = ADAPTER_SCALE * jnp.dot(low_rank_input.T, cotangent, preferred_element_type=jnp.float32) * gradient_norm
    grad_down = jnp.dot(acts.T, backward_result, preferred_element_type=jnp.float32) * gradient_norm
    width = KV // N_COL
    total = jnp.dot(backward_result, adapt_down.T, preferred_element_type=jnp.float32)
    for block in range(N_COL):
        part = jnp.dot(cotangent[:, block * width:(block + 1) * width], w_value[:, block * width:(block + 1) * width].T, preferred_element_type=jnp.float32)
        part = lax.optimization_barrier(part.astype(jnp.bfloat16))
        total = total + part.astype(jnp.float32)
    grad_acts = total.astype(jnp.bfloat16)
    return (values, grad_acts, grad_down, up_factor_gradient)
```

```python
import functools
import math

import jax
import jax.numpy as jnp
from jax import lax
from jax.experimental import pallas as pl
from jax.experimental.pallas import tpu as pltpu
from jax.sharding import PartitionSpec as P

ADAPTER_SCALE = 2.0
MESH = pl.DeviceIdType.MESH
F32 = jnp.float32
BF16 = jnp.bfloat16


def dot(a, b, da=1, db=0):
    return lax.dot_general(a, b, (((da,), (db,)), ((), ())), preferred_element_type=F32)


def exchange_kernel(
    nz,
    norm,
    acts,
    w,
    down_t,
    up,
    cot,
    values,
    gacts,
    gdown,
    gup,
    xa,
    ct,
    uf,
    df,
    wf,
    gds,
    gdr,
    lows,
    lowr,
    ups,
    upx,
    upz,
    upd,
    gas,
    vs,
    vr,
    vacc,
    s_acts,
    r_acts,
    s_cot,
    r_cot,
    s_up,
    r_up,
    s_dn,
    r_dn,
    s_w,
    r_w,
    s_wl,
    r_wl,
    s_f,
    r_f,
    s_gd,
    r_gd,
    s_low,
    r_low,
    s_ux,
    r_ux,
    s_uz,
    r_uz,
    s_ud,
    r_ud,
    s_ga,
    r_ga,
    s_v,
    r_v,
):
    y, row, c = lax.axis_index("groups"), lax.axis_index("row"), lax.axis_index("col")
    z, x = row // 2, row % 2
    tok, depth, feat = acts.shape[0], w.shape[0], w.shape[1]
    rank = up.shape[0]
    half, hr = depth // 2, rank // 2
    blocks = nz // 2
    home, place = z // blocks, z % blocks
    xo, co, yo = 1 - x, 1 - c, 1 - y

    def dev(yy, zz, xx, cc):
        return (yy, zz * 2 + xx, cc)

    def cols(i, n):
        return pl.ds(pl.multiple_of(i * n, n), n)

    def rc(src, dst, ss, rs, to):
        return pltpu.make_async_remote_copy(
            src_ref=src, dst_ref=dst, send_sem=ss, recv_sem=rs, device_id=to, device_id_type=MESH
        )

    other = dev(y, z, xo, c)

    def arrived(dst, rs):
        rc(dst, dst, rs, rs, other).wait_recv()

    mates = [(x, co), (xo, c), (xo, co)]
    zs = [lax.rem(z + k, nz) for k in range(1, nz)]

    barrier = pltpu.get_barrier_semaphore()
    peers = [dev(y, z, a, b) for a, b in mates] + [dev(yo, z, x, c)]
    peers += [dev(y, t, x, b) for t in zs for b in range(2)]
    for p in peers:
        pl.semaphore_signal(barrier, inc=1, device_id=p, device_id_type=MESH)
    pl.semaphore_wait(barrier, len(peers))

    sent = []

    mine = (cols(x, tok), cols(c, feat))
    for i, (a, b) in enumerate(mates):
        cp = rc(cot, ct.at[mine], s_cot.at[i], r_cot.at[x * 2 + c], dev(y, z, a, b))
        cp.start()
        sent.append(cp)
    cp = rc(up, uf.at[:, cols(c, feat)], s_up, r_up, dev(y, z, x, co))
    cp.start()
    sent.append(cp)
    for b in range(blocks):
        cp = rc(
            acts.at[:, cols(b * 2 + xo, depth)],
            xa.at[b, cols(x, tok), :],
            s_acts.at[b],
            r_acts.at[b],
            other,
        )
        cp.start()
        sent.append(cp)

    dn_copies = [
        rc(down_t, df.at[place], s_dn.at[k], r_dn.at[place], dev(y, t, x, c))
        for k, t in enumerate(zs)
    ]

    @pl.when(c == home)
    def _():
        for cp in dn_copies:
            cp.start()

    w_local = rc(w, wf.at[place, :, cols(c, feat)], s_wl, r_wl, dev(y, z, x, co))

    for k, t in enumerate(zs):
        cp = rc(
            w.at[cols(y, half), :],
            wf.at[place, cols(y, half), cols(c, feat)],
            s_w.at[k],
            r_w.at[place, c],
            dev(y, t, x, home),
        )
        cp.start()
        sent.append(cp)

    @pl.when(c != home)
    def _():
        w_local.start()

    ct[mine] = cot[...]
    uf[:, cols(c, feat)] = up[...]
    for b in range(blocks):
        xa[b, cols(x, tok), :] = acts[:, cols(b * 2 + x, depth)]

    @pl.when(c == home)
    def _():
        df[place] = down_t[...]
        wf[place, :, cols(c, feat)] = w[...]

    for a, b in mates:
        arrived(ct.at[cols(a, tok), cols(b, feat)], r_cot.at[a * 2 + b])
    arrived(uf.at[:, cols(co, feat)], r_up)
    back = (ADAPTER_SCALE * dot(ct[...], uf[...], 1, 1)).astype(BF16)
    gd_copies = []
    for b in range(blocks):
        arrived(xa.at[b, cols(xo, tok), :], r_acts.at[b])
        gds[b] = dot(back, xa[b], 0, 0)
        t = c * blocks + b
        for e in range(2):
            cp = rc(
                gds.at[b, :, pl.ds(e * half, half)],
                gdr.at[z],
                s_gd.at[b, e],
                r_gd.at[z],
                dev(y, t, x, e),
            )
            here = (t == z) & (c == e)
            gd_copies.append((here, cp))

            @pl.when(here)
            def _():
                gdr[z] = gds[b, :, e * half : (e + 1) * half]

            @pl.when(jnp.logical_not(here))
            def _():
                cp.start()

    low_t = jnp.zeros((rank, 2 * tok), F32)
    for b in range(blocks):

        @pl.when(c * blocks + b != z)
        def _():
            arrived(df.at[b], r_dn.at[b])

        low_t += dot(df[b], xa[b], 1, 1)
    lows[0] = low_t[:, :tok]
    lows[1] = low_t[:, tok:]
    for i, (a, b) in enumerate(mates):
        cp = rc(lows.at[a], lowr.at[x * 2 + c], s_low.at[i], r_low.at[x * 2 + c], dev(y, z, a, b))
        cp.start()
        sent.append(cp)
    low = lows[x]
    for a, b in mates:
        arrived(lowr.at[a * 2 + b], r_low.at[a * 2 + b])
        low += lowr[a * 2 + b]
    low = low.astype(BF16)

    ups[...] = ADAPTER_SCALE * dot(low, ct[mine])
    cp = rc(ups.at[cols(xo, hr), :], upx, s_ux, r_ux, other)
    cp.start()
    sent.append(cp)
    arrived(upx, r_ux)
    upz[z] = ups[cols(x, hr), :] + upx[...]
    for k, t in enumerate(zs):
        cp = rc(upz.at[z], upz.at[z], s_uz.at[k], r_uz.at[z], dev(y, t, x, c))
        cp.start()
        sent.append(cp)

    order = [lax.rem(place + b, blocks) for b in range(blocks)]
    forwards = []
    for b in order:
        absent = c * blocks + b != z
        for e in range(2):
            piece = wf.at[b, cols(y, half), pl.ds(e * feat, feat)]
            cp = rc(piece, piece, s_f.at[b, e], r_f.at[b, e], dev(yo, z, x, c))
            forwards.append((absent, cp))

            @pl.when(absent)
            def _():
                arrived(piece, r_w.at[b, e])
                cp.start()

    for t in zs:
        arrived(upz.at[t], r_uz.at[t])
    total = upz[0]
    for t in range(1, nz):
        total += upz[t]
    upd[...] = total * norm
    gup[cols(x, hr), :] = upd[...]
    cp = rc(upd, gup.at[cols(x, hr), :], s_ud, r_ud, other)
    cp.start()
    sent.append(cp)

    for t in zs:
        arrived(gdr.at[t], r_gd.at[t])

    @pl.when(c != home)
    def _():
        arrived(gdr.at[z], r_gd.at[z])

    total = gdr[0]
    for t in range(1, nz):
        total += gdr[t]
    gdown[...] = (total * norm).T

    for i, b in enumerate(order):
        absent = c * blocks + b != z

        @pl.when(absent)
        def _():
            for e in range(2):
                arrived(wf.at[b, cols(yo, half), pl.ds(e * feat, feat)], r_f.at[b, e])

        @pl.when(jnp.logical_not(absent))
        def _():
            arrived(wf.at[b, :, cols(co, feat)], r_wl)

        grad = dot(back, df[b])
        for e in range(2):
            part = dot(ct[:, e * feat : (e + 1) * feat], wf[b, :, e * feat : (e + 1) * feat], 1, 1)
            grad += part.astype(BF16).astype(F32)
        gas[i] = grad.astype(BF16)
        block = cols(b * 2 + x, depth)
        cp = rc(
            gas.at[i, cols(xo, tok), :], gacts.at[:, block], s_ga.at[b], r_ga.at[b], other
        )
        cp.start()
        sent.append(cp)
        part = dot(xa[b], wf[b])
        if i == 0:
            vacc[...] = part
        else:
            vacc[...] += part
        gacts[:, block] = gas[i, cols(x, tok), :]

    vs[...] = vacc[...].astype(BF16)
    for i, (a, b) in enumerate(mates):
        cp = rc(
            vs.at[cols(a, tok), cols(b, feat)],
            vr.at[x * 2 + c],
            s_v.at[i],
            r_v.at[x * 2 + c],
            dev(y, z, a, b),
        )
        cp.start()
        sent.append(cp)
    out = vacc[mine] + ADAPTER_SCALE * dot(low, up[...], 0, 0)
    for a, b in mates:
        arrived(vr.at[a * 2 + b], r_v.at[a * 2 + b])
        out += vr[a * 2 + b].astype(F32)
    values[...] = out.astype(BF16)

    arrived(gup.at[cols(xo, hr), :], r_ud)
    for b in range(blocks):
        arrived(gacts.at[:, cols(b * 2 + xo, depth)], r_ga.at[b])
    for cp in sent:
        cp.wait_send()
    for here, cp in gd_copies:

        @pl.when(jnp.logical_not(here))
        def _():
            cp.wait_send()

    for absent, cp in forwards:

        @pl.when(absent)
        def _():
            cp.wait_send()

    @pl.when(c == home)
    def _():
        for cp in dn_copies:
            cp.wait_send()

    @pl.when(c != home)
    def _():
        w_local.wait_send()


def kernel_body(acts, w_value, adapt_down, adapter_up_factor, cotangent):
    tok, width = acts.shape
    depth, feat = w_value.shape
    rank = adapter_up_factor.shape[0]
    rows = lax.axis_size("row")
    nz = rows // 2
    blocks, half, hr = nz // 2, depth // 2, rank // 2
    norm = 1.0 / math.sqrt(tok * rows)
    vmem = pl.BlockSpec(memory_space=pltpu.VMEM)
    dma = lambda *s: pltpu.SemaphoreType.DMA(s) if s else pltpu.SemaphoreType.DMA
    scratch = [
        pltpu.VMEM((blocks, 2 * tok, depth), BF16),
        pltpu.VMEM((2 * tok, 2 * feat), BF16),
        pltpu.VMEM((rank, 2 * feat), BF16),
        pltpu.VMEM((blocks, rank, depth), BF16),
        pltpu.VMEM((blocks, depth, 2 * feat), BF16),
        pltpu.VMEM((blocks, rank, depth), F32),
        pltpu.VMEM((nz, rank, half), F32),
        pltpu.VMEM((2, rank, tok), F32),
        pltpu.VMEM((4, rank, tok), F32),
        pltpu.VMEM((rank, feat), F32),
        pltpu.VMEM((hr, feat), F32),
        pltpu.VMEM((nz, hr, feat), F32),
        pltpu.VMEM((hr, feat), F32),
        pltpu.VMEM((blocks, 2 * tok, depth), BF16),
        pltpu.VMEM((2 * tok, 2 * feat), BF16),
        pltpu.VMEM((4, tok, feat), BF16),
        pltpu.VMEM((2 * tok, 2 * feat), F32),
        dma(blocks), dma(blocks),
        dma(3), dma(4),
        dma(), dma(),
        dma(nz - 1), dma(blocks),
        dma(nz - 1), dma(blocks, 2),
        dma(), dma(),
        dma(blocks, 2), dma(blocks, 2),
        dma(blocks, 2), dma(nz),
        dma(3), dma(4),
        dma(), dma(),
        dma(nz - 1), dma(nz),
        dma(), dma(),
        dma(blocks), dma(blocks),
        dma(3), dma(4),
    ]
    return pl.pallas_call(
        functools.partial(exchange_kernel, nz, norm),
        out_shape=(
            jax.ShapeDtypeStruct((tok, feat), BF16),
            jax.ShapeDtypeStruct((tok, width), BF16),
            jax.ShapeDtypeStruct((half, rank), F32),
            jax.ShapeDtypeStruct((rank, feat), F32),
        ),
        in_specs=[vmem] * 5,
        out_specs=(vmem,) * 4,
        scratch_shapes=scratch,
        compiler_params=pltpu.CompilerParams(
            collective_id=0, has_side_effects=True, vmem_limit_bytes=48 * 2**20
        ),
    )(acts, w_value, adapt_down.T, adapter_up_factor, cotangent)


def body(acts, w_value, adapt_down, adapter_up_factor, cotangent):
    whole = lax.all_gather(acts, "col", axis=1, tiled=True)
    tok_count = whole.shape[0]
    width = whole.shape[1]
    down_full = lax.all_gather(adapt_down, "row", axis=0, tiled=True)
    piece = lax.all_gather(w_value, "row", axis=0, tiled=True)
    span = whole
    base_output = jnp.dot(span, piece, preferred_element_type=jnp.float32)
    base_output, stored = (base_output, piece)
    low_sum = jnp.dot(whole, down_full, preferred_element_type=jnp.float32)
    low_rank_input = low_sum.astype(jnp.bfloat16)
    values = (
        base_output
        + ADAPTER_SCALE
        * jnp.dot(low_rank_input, adapter_up_factor, preferred_element_type=jnp.float32)
    ).astype(jnp.bfloat16)
    backward_piece = ADAPTER_SCALE * jnp.dot(
        cotangent, adapter_up_factor.T, preferred_element_type=jnp.float32
    )
    backward_result = lax.psum(backward_piece.astype(jnp.bfloat16), "col")
    total_tokens = tok_count * lax.axis_size("row")
    gradient_norm = 1.0 / math.sqrt(total_tokens)
    up_factor_piece = ADAPTER_SCALE * jnp.dot(
        low_rank_input.T, cotangent, preferred_element_type=jnp.float32
    )
    up_factor_gradient = lax.psum(up_factor_piece, "row") * gradient_norm
    col_index = lax.axis_index("col")
    pair_count = lax.axis_size("col")
    tok_half = tok_count // pair_count
    mine_acts = lax.dynamic_slice_in_dim(whole, col_index * tok_half, tok_half, 0)
    mine_back = lax.dynamic_slice_in_dim(backward_result, col_index * tok_half, tok_half, 0)
    span = mine_acts
    grad_down = (
        lax.psum_scatter(
            jnp.dot(span.T, mine_back, preferred_element_type=jnp.float32),
            ("row", "col"),
            scatter_dimension=0,
            tiled=True,
        )
        * gradient_norm
    )
    d_half = width // pair_count
    down_mine = lax.dynamic_slice_in_dim(down_full, col_index * d_half, d_half, 0)
    adapter_dx = jnp.dot(backward_result, down_mine.T, preferred_element_type=jnp.float32)
    partial_dx = jnp.dot(cotangent, stored.T, preferred_element_type=jnp.float32)
    base_dx = lax.psum_scatter(
        partial_dx.astype(jnp.bfloat16), "col", scatter_dimension=1, tiled=True
    ).astype(jnp.float32)
    grad_acts = (base_dx + adapter_dx).astype(jnp.bfloat16)
    return (values, grad_acts, grad_down, up_factor_gradient)


def pick(mesh, *arrays):
    rows, tiles = lax.axis_size("row"), arrays[1].shape[0] % 256 == 0
    fits = rows % 4 == 0 and mesh.shape["groups"] == 2 and mesh.shape["col"] == 2
    step = kernel_body if fits and tiles else body
    return step(*arrays)


def solution(mesh):
    return jax.shard_map(
        functools.partial(pick, mesh),
        mesh=mesh,
        in_specs=(
            P(("groups", "row"), "col"),
            P("row", "col"),
            P("row", None),
            P(None, "col"),
            P(("groups", "row"), "col"),
        ),
        out_specs=(
            P(("groups", "row"), "col"),
            P(("groups", "row"), "col"),
            P(("groups", "row", "col"), None),
            P("groups", "col"),
        ),
        check_vma=False,
    )
```

```python
import functools
import math

import jax
import jax.numpy as jnp
from jax import lax
from jax.experimental import pallas as pl
from jax.experimental.pallas import tpu as pltpu
from jax.sharding import PartitionSpec as P

ADAPTER_SCALE = 2.0
MESH = pl.DeviceIdType.MESH
PIECES = 2
F32 = jnp.float32
BF16 = jnp.bfloat16


def dot(a, b, da=1, db=0):
    return lax.dot_general(a, b, (((da,), (db,)), ((), ())), preferred_element_type=F32)


def exchange_kernel(
    nz,
    norm,
    acts,
    w,
    down_t,
    up,
    cot,
    values,
    gacts,
    gdown,
    gup,
    xa,
    ct,
    uf,
    df,
    wf,
    gds,
    gdr,
    lows,
    lowr,
    ups,
    upx,
    upz,
    upd,
    gas,
    vs,
    vr,
    vacc,
    s_acts,
    r_acts,
    s_cot,
    r_cot,
    s_up,
    r_up,
    s_dn,
    r_dn,
    s_w,
    r_w,
    s_wl,
    r_wl,
    s_f,
    r_f,
    s_h,
    s_in,
    s_gd,
    r_gd,
    s_low,
    r_low,
    s_ux,
    r_ux,
    s_uz,
    r_uz,
    s_ud,
    r_ud,
    s_ga,
    r_ga,
    s_v,
    r_v,
):
    y, row, c = lax.axis_index("groups"), lax.axis_index("row"), lax.axis_index("col")
    z, x = row // 2, row % 2
    tok, depth, feat = acts.shape[0], w.shape[0], w.shape[1]
    rank = up.shape[0]
    half, hr = depth // 2, rank // 2
    rows = half // PIECES
    blocks = nz // 2
    home, place = z // blocks, z % blocks
    xo, co, yo = 1 - x, 1 - c, 1 - y

    def dev(yy, zz, xx, cc):
        return (yy, zz * 2 + xx, cc)

    def cols(i, n):
        return pl.ds(pl.multiple_of(i * n, n), n)

    def rc(src, dst, ss, rs, to):
        return pltpu.make_async_remote_copy(
            src_ref=src, dst_ref=dst, send_sem=ss, recv_sem=rs, device_id=to, device_id_type=MESH
        )

    other = dev(y, z, xo, c)

    def arrived(dst, rs):
        rc(dst, dst, rs, rs, other).wait_recv()

    mates = [(x, co), (xo, c), (xo, co)]
    zs = [lax.rem(z + k, nz) for k in range(1, nz)]

    barrier = pltpu.get_barrier_semaphore()
    peers = [dev(y, z, a, b) for a, b in mates] + [dev(yo, z, x, c)]
    peers += [dev(y, t, x, b) for t in zs for b in range(2)]
    for p in peers:
        pl.semaphore_signal(barrier, inc=1, device_id=p, device_id_type=MESH)
    pl.semaphore_wait(barrier, len(peers))

    sent = []

    mine = (cols(x, tok), cols(c, feat))
    for i, (a, b) in enumerate(mates):
        cp = rc(cot, ct.at[mine], s_cot.at[i], r_cot.at[x * 2 + c], dev(y, z, a, b))
        cp.start()
        sent.append(cp)
    cp = rc(up, uf.at[:, cols(c, feat)], s_up, r_up, dev(y, z, x, co))
    cp.start()
    sent.append(cp)
    for b in range(blocks):
        cp = rc(
            acts.at[:, cols(b * 2 + xo, depth)],
            xa.at[b, cols(x, tok), :],
            s_acts.at[b],
            r_acts.at[b],
            other,
        )
        cp.start()
        sent.append(cp)

    dn_copies = [
        rc(down_t, df.at[place], s_dn.at[k], r_dn.at[place], dev(y, t, x, c))
        for k, t in enumerate(zs)
    ]

    @pl.when(c == home)
    def _():
        for cp in dn_copies:
            cp.start()

    w_local = rc(w, wf.at[place, :, cols(c, feat)], s_wl, r_wl, dev(y, z, x, co))

    own_sends = []
    for i, t in enumerate((z + 1, z - 1)):
        there = (t >= 0) & (t < nz)
        for q in range(PIECES):
            piece = cols(y * PIECES + q, rows)
            cp = rc(
                w.at[piece, :],
                wf.at[place, piece, cols(c, feat)],
                s_w.at[i, q],
                r_w.at[place, c, q],
                dev(y, jnp.clip(t, 0, nz - 1), x, home),
            )
            own_sends.append((there, cp))

            @pl.when(there)
            def _():
                cp.start()

    @pl.when(c != home)
    def _():
        w_local.start()

    into = [
        pltpu.make_async_copy(cot, ct.at[mine], s_in.at[0]),
        pltpu.make_async_copy(up, uf.at[:, cols(c, feat)], s_in.at[1]),
    ]
    for b in range(blocks):
        into.append(
            pltpu.make_async_copy(
                acts.at[:, cols(b * 2 + x, depth)], xa.at[b, cols(x, tok), :], s_in.at[4 + b]
            )
        )
    into_home = [
        pltpu.make_async_copy(down_t, df.at[place], s_in.at[2]),
        pltpu.make_async_copy(w, wf.at[place, :, cols(c, feat)], s_in.at[3]),
    ]
    for cp in into:
        cp.start()

    @pl.when(c == home)
    def _():
        for cp in into_home:
            cp.start()

    def in_order(i, first):
        return jnp.where(
            c == home, lax.rem(place + first + i, blocks), jnp.where(c > home, i, blocks - 1 - i)
        )

    forwards = []

    def pass_on(b):
        source = c * blocks + b
        absent = source != z
        t = jnp.where(source < z, z + 1, z - 1)
        more = absent & (t >= 0) & (t < nz)
        for q in range(PIECES):
            for e in range(2):
                piece = wf.at[b, cols(y * PIECES + q, rows), pl.ds(e * feat, feat)]
                hop = rc(
                    piece,
                    piece,
                    s_h.at[b, e, q],
                    r_w.at[b, e, q],
                    dev(y, jnp.clip(t, 0, nz - 1), x, c),
                )
                side = rc(piece, piece, s_f.at[b, e, q], r_f.at[b, e, q], dev(yo, z, x, c))
                forwards.append((more, hop))
                forwards.append((absent, side))

                @pl.when(absent)
                def _():
                    arrived(piece, r_w.at[b, e, q])

                @pl.when(more)
                def _():
                    hop.start()

                @pl.when(absent)
                def _():
                    side.start()

    pass_on(in_order(0, 1))

    for cp in into:
        cp.wait()

    @pl.when(c == home)
    def _():
        for cp in into_home:
            cp.wait()

    for a, b in mates:
        arrived(ct.at[cols(a, tok), cols(b, feat)], r_cot.at[a * 2 + b])
    arrived(uf.at[:, cols(co, feat)], r_up)
    back = (ADAPTER_SCALE * dot(ct[...], uf[...], 1, 1)).astype(BF16)
    gd_copies = []
    for b in range(blocks):
        arrived(xa.at[b, cols(xo, tok), :], r_acts.at[b])
        gds[b] = dot(back, xa[b], 0, 0).astype(BF16)
        t = c * blocks + b
        for e in range(2):
            cp = rc(
                gds.at[b, :, pl.ds(e * half, half)],
                gdr.at[z],
                s_gd.at[b, e],
                r_gd.at[z],
                dev(y, t, x, e),
            )
            here = (t == z) & (c == e)
            gd_copies.append((here, cp))

            @pl.when(here)
            def _():
                gdr[z] = gds[b, :, e * half : (e + 1) * half]

            @pl.when(jnp.logical_not(here))
            def _():
                cp.start()

    low_t = jnp.zeros((rank, 2 * tok), F32)
    for b in range(blocks):

        @pl.when(c * blocks + b != z)
        def _():
            arrived(df.at[b], r_dn.at[b])

        low_t += dot(df[b], xa[b], 1, 1)
    lows[0] = low_t[:, :tok]
    lows[1] = low_t[:, tok:]
    for i, (a, b) in enumerate(mates):
        cp = rc(lows.at[a], lowr.at[x * 2 + c], s_low.at[i], r_low.at[x * 2 + c], dev(y, z, a, b))
        cp.start()
        sent.append(cp)
    def work_on(b, first):
        absent = c * blocks + b != z

        @pl.when(jnp.logical_not(absent))
        def _():
            arrived(wf.at[b, :, cols(co, feat)], r_wl)

        for q in range(PIECES):
            for h in (y, yo):
                chunk = cols(h * PIECES + q, rows)
                if h is yo:

                    @pl.when(absent)
                    def _():
                        for e in range(2):
                            arrived(wf.at[b, chunk, pl.ds(e * feat, feat)], r_f.at[b, e, q])

                part = dot(xa[b, :, chunk], wf[b, chunk, :])
                if first and q == 0 and h is y:
                    vacc[...] = part
                else:
                    vacc[...] += part
                grad = dot(back, df[b, :, chunk])
                for e in range(2):
                    part = dot(
                        ct[:, e * feat : (e + 1) * feat],
                        wf[b, chunk, e * feat : (e + 1) * feat],
                        1,
                        1,
                    )
                    grad += part.astype(BF16).astype(F32)
                gas[b, :, chunk] = grad.astype(BF16)
                place_of = cols(((b * 2 + x) * 2 + h) * PIECES + q, rows)
                cp = rc(
                    gas.at[b, cols(xo, tok), chunk],
                    gacts.at[:, place_of],
                    s_ga.at[b, h, q],
                    r_ga.at[b, h, q],
                    other,
                )
                cp.start()
                sent.append(cp)
                gacts[:, place_of] = gas[b, cols(x, tok), chunk]

    work_on(in_order(0, 0), True)

    low = lows[x]
    for a, b in mates:
        arrived(lowr.at[a * 2 + b], r_low.at[a * 2 + b])
        low += lowr[a * 2 + b]
    low = low.astype(BF16)

    ups[...] = ADAPTER_SCALE * dot(low, ct[mine])
    cp = rc(ups.at[cols(xo, hr), :], upx, s_ux, r_ux, other)
    cp.start()
    sent.append(cp)
    arrived(upx, r_ux)
    upz[z] = ups[cols(x, hr), :] + upx[...]
    for k, t in enumerate(zs):
        cp = rc(upz.at[z], upz.at[z], s_uz.at[k], r_uz.at[z], dev(y, t, x, c))
        cp.start()
        sent.append(cp)

    for i in range(1, blocks):
        pass_on(in_order(i, 1))

    for t in zs:
        arrived(upz.at[t], r_uz.at[t])
    total = upz[0]
    for t in range(1, nz):
        total += upz[t]
    upd[...] = total * norm
    gup[cols(x, hr), :] = upd[...]
    cp = rc(upd, gup.at[cols(x, hr), :], s_ud, r_ud, other)
    cp.start()
    sent.append(cp)

    for t in zs:
        arrived(gdr.at[t], r_gd.at[t])

    @pl.when(c != home)
    def _():
        arrived(gdr.at[z], r_gd.at[z])

    total = gdr[0].astype(F32)
    for t in range(1, nz):
        total += gdr[t].astype(F32)
    gdown[...] = total * norm

    for i in range(1, blocks):
        work_on(in_order(i, 0), False)

    vs[...] = vacc[...].astype(BF16)
    for i, (a, b) in enumerate(mates):
        cp = rc(
            vs.at[cols(a, tok), cols(b, feat)],
            vr.at[x * 2 + c],
            s_v.at[i],
            r_v.at[x * 2 + c],
            dev(y, z, a, b),
        )
        cp.start()
        sent.append(cp)
    out = vacc[mine] + ADAPTER_SCALE * dot(low, uf[:, cols(c, feat)], 0, 0)
    for a, b in mates:
        arrived(vr.at[a * 2 + b], r_v.at[a * 2 + b])
        out += vr[a * 2 + b].astype(F32)
    values[...] = out.astype(BF16)

    arrived(gup.at[cols(xo, hr), :], r_ud)
    for b in range(blocks):
        for h in range(2):
            for q in range(PIECES):
                at = cols(((b * 2 + xo) * 2 + h) * PIECES + q, rows)
                arrived(gacts.at[:, at], r_ga.at[b, h, q])
    for cp in sent:
        cp.wait_send()
    for here, cp in gd_copies:

        @pl.when(jnp.logical_not(here))
        def _():
            cp.wait_send()

    for used, cp in own_sends + forwards:

        @pl.when(used)
        def _():
            cp.wait_send()

    @pl.when(c == home)
    def _():
        for cp in dn_copies:
            cp.wait_send()

    @pl.when(c != home)
    def _():
        w_local.wait_send()


def kernel_body(acts, w_value, adapt_down, adapter_up_factor, cotangent):
    tok, width = acts.shape
    depth, feat = w_value.shape
    rank = adapter_up_factor.shape[0]
    rows = lax.axis_size("row")
    nz = rows // 2
    blocks, half, hr = nz // 2, depth // 2, rank // 2
    norm = 1.0 / math.sqrt(tok * rows)
    vmem = pl.BlockSpec(memory_space=pltpu.VMEM)
    dma = lambda *s: pltpu.SemaphoreType.DMA(s) if s else pltpu.SemaphoreType.DMA
    scratch = [
        pltpu.VMEM((blocks, 2 * tok, depth), BF16),
        pltpu.VMEM((2 * tok, 2 * feat), BF16),
        pltpu.VMEM((rank, 2 * feat), BF16),
        pltpu.VMEM((blocks, rank, depth), BF16),
        pltpu.VMEM((blocks, depth, 2 * feat), BF16),
        pltpu.VMEM((blocks, rank, depth), BF16),
        pltpu.VMEM((nz, rank, half), BF16),
        pltpu.VMEM((2, rank, tok), F32),
        pltpu.VMEM((4, rank, tok), F32),
        pltpu.VMEM((rank, feat), F32),
        pltpu.VMEM((hr, feat), F32),
        pltpu.VMEM((nz, hr, feat), F32),
        pltpu.VMEM((hr, feat), F32),
        pltpu.VMEM((blocks, 2 * tok, depth), BF16),
        pltpu.VMEM((2 * tok, 2 * feat), BF16),
        pltpu.VMEM((4, tok, feat), BF16),
        pltpu.VMEM((2 * tok, 2 * feat), F32),
        dma(blocks), dma(blocks),
        dma(3), dma(4),
        dma(), dma(),
        dma(nz - 1), dma(blocks),
        dma(2, PIECES), dma(blocks, 2, PIECES),
        dma(), dma(),
        dma(blocks, 2, PIECES), dma(blocks, 2, PIECES),
        dma(blocks, 2, PIECES), dma(4 + blocks),
        dma(blocks, 2), dma(nz),
        dma(3), dma(4),
        dma(), dma(),
        dma(nz - 1), dma(nz),
        dma(), dma(),
        dma(blocks, 2, PIECES), dma(blocks, 2, PIECES),
        dma(3), dma(4),
    ]
    values, grad_acts, grad_down_t, grad_up = pl.pallas_call(
        functools.partial(exchange_kernel, nz, norm),
        out_shape=(
            jax.ShapeDtypeStruct((tok, feat), BF16),
            jax.ShapeDtypeStruct((tok, width), BF16),
            jax.ShapeDtypeStruct((rank, half), F32),
            jax.ShapeDtypeStruct((rank, feat), F32),
        ),
        in_specs=[pl.BlockSpec(memory_space=pltpu.HBM)] * 5,
        out_specs=(vmem,) * 4,
        scratch_shapes=scratch,
        compiler_params=pltpu.CompilerParams(
            collective_id=0, has_side_effects=True, vmem_limit_bytes=48 * 2**20
        ),
    )(acts, w_value, adapt_down.T, adapter_up_factor, cotangent)
    return values, grad_acts, grad_down_t.T, grad_up


def body(acts, w_value, adapt_down, adapter_up_factor, cotangent):
    whole = lax.all_gather(acts, "col", axis=1, tiled=True)
    tok_count = whole.shape[0]
    width = whole.shape[1]
    down_full = lax.all_gather(adapt_down, "row", axis=0, tiled=True)
    piece = lax.all_gather(w_value, "row", axis=0, tiled=True)
    span = whole
    base_output = jnp.dot(span, piece, preferred_element_type=jnp.float32)
    base_output, stored = (base_output, piece)
    low_sum = jnp.dot(whole, down_full, preferred_element_type=jnp.float32)
    low_rank_input = low_sum.astype(jnp.bfloat16)
    values = (
        base_output
        + ADAPTER_SCALE
        * jnp.dot(low_rank_input, adapter_up_factor, preferred_element_type=jnp.float32)
    ).astype(jnp.bfloat16)
    backward_piece = ADAPTER_SCALE * jnp.dot(
        cotangent, adapter_up_factor.T, preferred_element_type=jnp.float32
    )
    backward_result = lax.psum(backward_piece.astype(jnp.bfloat16), "col")
    total_tokens = tok_count * lax.axis_size("row")
    gradient_norm = 1.0 / math.sqrt(total_tokens)
    up_factor_piece = ADAPTER_SCALE * jnp.dot(
        low_rank_input.T, cotangent, preferred_element_type=jnp.float32
    )
    up_factor_gradient = lax.psum(up_factor_piece, "row") * gradient_norm
    col_index = lax.axis_index("col")
    pair_count = lax.axis_size("col")
    tok_half = tok_count // pair_count
    mine_acts = lax.dynamic_slice_in_dim(whole, col_index * tok_half, tok_half, 0)
    mine_back = lax.dynamic_slice_in_dim(backward_result, col_index * tok_half, tok_half, 0)
    span = mine_acts
    grad_down = (
        lax.psum_scatter(
            jnp.dot(span.T, mine_back, preferred_element_type=jnp.float32),
            ("row", "col"),
            scatter_dimension=0,
            tiled=True,
        )
        * gradient_norm
    )
    d_half = width // pair_count
    down_mine = lax.dynamic_slice_in_dim(down_full, col_index * d_half, d_half, 0)
    adapter_dx = jnp.dot(backward_result, down_mine.T, preferred_element_type=jnp.float32)
    partial_dx = jnp.dot(cotangent, stored.T, preferred_element_type=jnp.float32)
    base_dx = lax.psum_scatter(
        partial_dx.astype(jnp.bfloat16), "col", scatter_dimension=1, tiled=True
    ).astype(jnp.float32)
    grad_acts = (base_dx + adapter_dx).astype(jnp.bfloat16)
    return (values, grad_acts, grad_down, up_factor_gradient)


def pick(mesh, *arrays):
    rows, tiles = lax.axis_size("row"), arrays[1].shape[0] % (512 * PIECES // 2) == 0
    fits = rows % 4 == 0 and mesh.shape["groups"] == 2 and mesh.shape["col"] == 2
    step = kernel_body if fits and tiles else body
    return step(*arrays)


def solution(mesh):
    return jax.shard_map(
        functools.partial(pick, mesh),
        mesh=mesh,
        in_specs=(
            P(("groups", "row"), "col"),
            P("row", "col"),
            P("row", None),
            P(None, "col"),
            P(("groups", "row"), "col"),
        ),
        out_specs=(
            P(("groups", "row"), "col"),
            P(("groups", "row"), "col"),
            P(("groups", "row", "col"), None),
            P("groups", "col"),
        ),
        check_vma=False,
    )
```

```python
import functools
import math

import jax
import jax.numpy as jnp
from jax import lax
from jax.experimental import pallas as pl
from jax.experimental.pallas import tpu as pltpu
from jax.sharding import PartitionSpec as P

ADAPTER_SCALE = 2.0
MESH = pl.DeviceIdType.MESH
PIECES = 4
F32 = jnp.float32
BF16 = jnp.bfloat16


def dot(a, b, da=1, db=0):
    return lax.dot_general(a, b, (((da,), (db,)), ((), ())), preferred_element_type=F32)


def exchange_kernel(
    nz,
    norm,
    acts,
    w,
    down_t,
    up,
    cot,
    values,
    gacts,
    gdown,
    gup,
    xa,
    ct,
    uf,
    df,
    wf,
    gds,
    gdr,
    lows,
    lowr,
    ups,
    upx,
    upz,
    upd,
    gas,
    vs,
    vr,
    vacc,
    s_acts,
    r_acts,
    s_cot,
    r_cot,
    s_up,
    r_up,
    s_dn,
    r_dn,
    s_dh,
    s_df,
    r_df,
    s_w,
    r_w,
    s_wl,
    r_wl,
    s_f,
    r_f,
    s_h,
    s_in,
    s_gd,
    r_gd,
    s_low,
    r_low,
    s_ux,
    r_ux,
    s_uz,
    r_uz,
    s_ud,
    r_ud,
    s_ga,
    r_ga,
    s_v,
    r_v,
):
    y, row, c = lax.axis_index("groups"), lax.axis_index("row"), lax.axis_index("col")
    z, x = row // 2, row % 2
    tok, depth, feat = acts.shape[0], w.shape[0], w.shape[1]
    rank = up.shape[0]
    half, hr = depth // 2, rank // 2
    rows = half // PIECES
    dr = rank // 2
    blocks = nz // 2
    home, place = z // blocks, z % blocks
    xo, co, yo = 1 - x, 1 - c, 1 - y

    def dev(yy, zz, xx, cc):
        return (yy, zz * 2 + xx, cc)

    def cols(i, n):
        return pl.ds(pl.multiple_of(i * n, n), n)

    def rc(src, dst, ss, rs, to):
        return pltpu.make_async_remote_copy(
            src_ref=src, dst_ref=dst, send_sem=ss, recv_sem=rs, device_id=to, device_id_type=MESH
        )

    other = dev(y, z, xo, c)

    def arrived(dst, rs):
        rc(dst, dst, rs, rs, other).wait_recv()

    mates = [(x, co), (xo, c), (xo, co)]
    zs = [lax.rem(z + k, nz) for k in range(1, nz)]

    barrier = pltpu.get_barrier_semaphore()
    peers = [dev(y, z, a, b) for a, b in mates] + [dev(yo, z, x, c)]
    peers += [dev(y, t, x, b) for t in zs for b in range(2)]
    for p in peers:
        pl.semaphore_signal(barrier, inc=1, device_id=p, device_id_type=MESH)
    pl.semaphore_wait(barrier, len(peers))

    sent = []

    mine = (cols(x, tok), cols(c, feat))
    for i, (a, b) in enumerate(mates):
        cp = rc(cot, ct.at[mine], s_cot.at[i], r_cot.at[x * 2 + c], dev(y, z, a, b))
        cp.start()
        sent.append(cp)
    cp = rc(up, uf.at[:, cols(c, feat)], s_up, r_up, dev(y, z, x, co))
    cp.start()
    sent.append(cp)
    for b in range(blocks):
        cp = rc(
            acts.at[:, cols(b * 2 + xo, depth)],
            xa.at[b, cols(x, tok), :],
            s_acts.at[b],
            r_acts.at[b],
            other,
        )
        cp.start()
        sent.append(cp)

    w_local = rc(w, wf.at[place, :, cols(c, feat)], s_wl, r_wl, dev(y, z, x, co))
    steps = [(i, t, (t >= 0) & (t < nz)) for i, t in enumerate((z + 1, z - 1))]
    own_sends = []

    def send_if(used, cp):
        own_sends.append((used, cp))

        @pl.when(used)
        def _():
            cp.start()

    for i, t, there in steps:
        part = cols(y, dr)
        to = dev(y, jnp.clip(t, 0, nz - 1), x, c)
        send_if(
            there & (c == home),
            rc(down_t.at[part, :], df.at[place, part, :], s_dn.at[i], r_dn.at[place], to),
        )
    for q in range(PIECES):
        for i, t, there in steps:
            piece = cols(q * 2 + y, rows)
            to = dev(y, jnp.clip(t, 0, nz - 1), x, home)
            send_if(
                there,
                rc(
                    w.at[piece, :],
                    wf.at[place, piece, cols(c, feat)],
                    s_w.at[i, q],
                    r_w.at[place, c, q],
                    to,
                ),
            )

    @pl.when(c != home)
    def _():
        w_local.start()

    into = [
        pltpu.make_async_copy(cot, ct.at[mine], s_in.at[0]),
        pltpu.make_async_copy(up, uf.at[:, cols(c, feat)], s_in.at[1]),
    ]
    for b in range(blocks):
        into.append(
            pltpu.make_async_copy(
                acts.at[:, cols(b * 2 + x, depth)], xa.at[b, cols(x, tok), :], s_in.at[4 + b]
            )
        )
    into_home = [
        pltpu.make_async_copy(down_t, df.at[place], s_in.at[2]),
        pltpu.make_async_copy(w, wf.at[place, :, cols(c, feat)], s_in.at[3]),
    ]
    for cp in into:
        cp.start()

    @pl.when(c == home)
    def _():
        for cp in into_home:
            cp.start()

    def in_order(i, first):
        return jnp.where(
            c == home, lax.rem(place + first + i, blocks), jnp.where(c > home, i, blocks - 1 - i)
        )

    def pass_piece(b, piece, s_next, s_side, r_here, r_side):
        source = c * blocks + b
        absent = source != z
        t = jnp.where(source < z, z + 1, z - 1)
        more = absent & (t >= 0) & (t < nz)

        @pl.when(absent)
        def _():
            arrived(piece, r_here)

        send_if(more, rc(piece, piece, s_next, r_here, dev(y, jnp.clip(t, 0, nz - 1), x, c)))
        send_if(absent, rc(piece, piece, s_side, r_side, dev(yo, z, x, c)))

    def pass_down(b):
        piece = df.at[b, cols(y, dr), :]
        pass_piece(b, piece, s_dh.at[b], s_df.at[b], r_dn.at[b], r_df.at[b])

    def pass_on(b, q):
        for e in range(2):
            pass_piece(
                b,
                wf.at[b, cols(q * 2 + y, rows), pl.ds(e * feat, feat)],
                s_h.at[b, e, q],
                s_f.at[b, e, q],
                r_w.at[b, e, q],
                r_f.at[b, e, q],
            )

    pass_down(in_order(0, 1))
    for q in range(PIECES):
        pass_on(in_order(0, 1), q)
    for i in range(1, blocks):
        pass_down(in_order(i, 1))

    for cp in into:
        cp.wait()

    @pl.when(c == home)
    def _():
        for cp in into_home:
            cp.wait()

    for a, b in mates:
        arrived(ct.at[cols(a, tok), cols(b, feat)], r_cot.at[a * 2 + b])
    arrived(uf.at[:, cols(co, feat)], r_up)
    back = (ADAPTER_SCALE * dot(ct[...], uf[...], 1, 1)).astype(BF16)
    gd_copies = []
    for b in range(blocks):
        arrived(xa.at[b, cols(xo, tok), :], r_acts.at[b])
        gds[b] = dot(back, xa[b], 0, 0).astype(BF16)
        t = c * blocks + b
        for e in range(2):
            cp = rc(
                gds.at[b, :, pl.ds(e * half, half)],
                gdr.at[z],
                s_gd.at[b, e],
                r_gd.at[z],
                dev(y, t, x, e),
            )
            here = (t == z) & (c == e)
            gd_copies.append((here, cp))

            @pl.when(here)
            def _():
                gdr[z] = gds[b, :, e * half : (e + 1) * half]

            @pl.when(jnp.logical_not(here))
            def _():
                cp.start()

    low_t = jnp.zeros((rank, 2 * tok), F32)
    for b in range(blocks):

        @pl.when(c * blocks + b != z)
        def _():
            arrived(df.at[b, cols(yo, dr), :], r_df.at[b])

        low_t += dot(df[b], xa[b], 1, 1)
    lows[0] = low_t[:, :tok]
    lows[1] = low_t[:, tok:]
    for i, (a, b) in enumerate(mates):
        cp = rc(lows.at[a], lowr.at[x * 2 + c], s_low.at[i], r_low.at[x * 2 + c], dev(y, z, a, b))
        cp.start()
        sent.append(cp)
    def send_values():
        vs[...] = vacc[...].astype(BF16)
        for i, (a, b) in enumerate(mates):
            cp = rc(
                vs.at[cols(a, tok), cols(b, feat)],
                vr.at[x * 2 + c],
                s_v.at[i],
                r_v.at[x * 2 + c],
                dev(y, z, a, b),
            )
            cp.start()
            sent.append(cp)

    def work_on(i, q):
        b = in_order(i, 0)
        absent = c * blocks + b != z
        chunk = pl.ds(q * 2 * rows, 2 * rows)
        if q == 0:

            @pl.when(jnp.logical_not(absent))
            def _():
                arrived(wf.at[b, :, cols(co, feat)], r_wl)

        @pl.when(absent)
        def _():
            for e in range(2):
                arrived(wf.at[b, cols(q * 2 + yo, rows), pl.ds(e * feat, feat)], r_f.at[b, e, q])

        part = dot(xa[b, :, chunk], wf[b, chunk, :])
        if i == 0 and q == 0:
            vacc[...] = part
        else:
            vacc[...] += part
        if i == blocks - 1 and q == PIECES - 1:
            send_values()
        grad = dot(back, df[b, :, chunk])
        for e in range(2):
            part = dot(
                ct[:, e * feat : (e + 1) * feat], wf[b, chunk, e * feat : (e + 1) * feat], 1, 1
            )
            grad += part.astype(BF16).astype(F32)
        gas[b, :, chunk] = grad.astype(BF16)
        at = cols((b * 2 + x) * PIECES + q, 2 * rows)
        cp = rc(
            gas.at[b, cols(xo, tok), chunk], gacts.at[:, at], s_ga.at[b, q], r_ga.at[b, q], other
        )
        cp.start()
        sent.append(cp)
        gacts[:, at] = gas[b, cols(x, tok), chunk]

    def work_and_pass(i, q):
        work_on(i, q)
        if i + 1 < blocks:
            pass_on(in_order(i + 1, 1), q)

    work_and_pass(0, 0)

    low = lows[x]
    for a, b in mates:
        arrived(lowr.at[a * 2 + b], r_low.at[a * 2 + b])
        low += lowr[a * 2 + b]
    low = low.astype(BF16)

    ups[...] = ADAPTER_SCALE * dot(low, ct[mine])
    cp = rc(ups.at[cols(xo, hr), :], upx, s_ux, r_ux, other)
    cp.start()
    sent.append(cp)
    work_and_pass(0, 1)
    arrived(upx, r_ux)
    upz[z] = (ups[cols(x, hr), :] + upx[...]).astype(BF16)
    for k, t in enumerate(zs):
        cp = rc(upz.at[z], upz.at[z], s_uz.at[k], r_uz.at[z], dev(y, t, x, c))
        cp.start()
        sent.append(cp)

    for n in range(2, blocks * PIECES - 2):
        work_and_pass(n // PIECES, n % PIECES)

    for t in zs:
        arrived(upz.at[t], r_uz.at[t])
    total = upz[0].astype(F32)
    for t in range(1, nz):
        total += upz[t].astype(F32)
    upd[...] = total * norm
    gup[cols(x, hr), :] = upd[...]
    cp = rc(upd, gup.at[cols(x, hr), :], s_ud, r_ud, other)
    cp.start()
    sent.append(cp)

    for t in zs:
        arrived(gdr.at[t], r_gd.at[t])

    @pl.when(c != home)
    def _():
        arrived(gdr.at[z], r_gd.at[z])

    total = gdr[0].astype(F32)
    for t in range(1, nz):
        total += gdr[t].astype(F32)
    gdown[...] = total * norm

    for n in range(blocks * PIECES - 2, blocks * PIECES):
        work_and_pass(n // PIECES, n % PIECES)

    out = vacc[mine] + ADAPTER_SCALE * dot(low, uf[:, cols(c, feat)], 0, 0)
    for a, b in mates:
        arrived(vr.at[a * 2 + b], r_v.at[a * 2 + b])
        out += vr[a * 2 + b].astype(F32)
    values[...] = out.astype(BF16)

    arrived(gup.at[cols(xo, hr), :], r_ud)
    for b in range(blocks):
        for q in range(PIECES):
            at = cols((b * 2 + xo) * PIECES + q, 2 * rows)
            arrived(gacts.at[:, at], r_ga.at[b, q])
    for cp in sent:
        cp.wait_send()
    for here, cp in gd_copies:

        @pl.when(jnp.logical_not(here))
        def _():
            cp.wait_send()

    for used, cp in own_sends:

        @pl.when(used)
        def _():
            cp.wait_send()

    @pl.when(c != home)
    def _():
        w_local.wait_send()


def kernel_body(acts, w_value, adapt_down, adapter_up_factor, cotangent):
    tok, width = acts.shape
    depth, feat = w_value.shape
    rank = adapter_up_factor.shape[0]
    rows = lax.axis_size("row")
    nz = rows // 2
    blocks, half, hr = nz // 2, depth // 2, rank // 2
    norm = 1.0 / math.sqrt(tok * rows)
    vmem = pl.BlockSpec(memory_space=pltpu.VMEM)
    dma = lambda *s: pltpu.SemaphoreType.DMA(s) if s else pltpu.SemaphoreType.DMA
    scratch = [
        pltpu.VMEM((blocks, 2 * tok, depth), BF16),
        pltpu.VMEM((2 * tok, 2 * feat), BF16),
        pltpu.VMEM((rank, 2 * feat), BF16),
        pltpu.VMEM((blocks, rank, depth), BF16),
        pltpu.VMEM((blocks, depth, 2 * feat), BF16),
        pltpu.VMEM((blocks, rank, depth), BF16),
        pltpu.VMEM((nz, rank, half), BF16),
        pltpu.VMEM((2, rank, tok), F32),
        pltpu.VMEM((4, rank, tok), F32),
        pltpu.VMEM((rank, feat), F32),
        pltpu.VMEM((hr, feat), F32),
        pltpu.VMEM((nz, hr, feat), BF16),
        pltpu.VMEM((hr, feat), F32),
        pltpu.VMEM((blocks, 2 * tok, depth), BF16),
        pltpu.VMEM((2 * tok, 2 * feat), BF16),
        pltpu.VMEM((4, tok, feat), BF16),
        pltpu.VMEM((2 * tok, 2 * feat), F32),
        dma(blocks), dma(blocks),
        dma(3), dma(4),
        dma(), dma(),
        dma(2), dma(blocks), dma(blocks), dma(blocks), dma(blocks),
        dma(2, PIECES), dma(blocks, 2, PIECES),
        dma(), dma(),
        dma(blocks, 2, PIECES), dma(blocks, 2, PIECES),
        dma(blocks, 2, PIECES), dma(4 + blocks),
        dma(blocks, 2), dma(nz),
        dma(3), dma(4),
        dma(), dma(),
        dma(nz - 1), dma(nz),
        dma(), dma(),
        dma(blocks, PIECES), dma(blocks, PIECES),
        dma(3), dma(4),
    ]
    values, grad_acts, grad_down_t, grad_up = pl.pallas_call(
        functools.partial(exchange_kernel, nz, norm),
        out_shape=(
            jax.ShapeDtypeStruct((tok, feat), BF16),
            jax.ShapeDtypeStruct((tok, width), BF16),
            jax.ShapeDtypeStruct((rank, half), F32),
            jax.ShapeDtypeStruct((rank, feat), F32),
        ),
        in_specs=[pl.BlockSpec(memory_space=pltpu.HBM)] * 5,
        out_specs=(vmem,) * 4,
        scratch_shapes=scratch,
        compiler_params=pltpu.CompilerParams(
            collective_id=0, has_side_effects=True, vmem_limit_bytes=62 * 2**20
        ),
    )(acts, w_value, adapt_down.T, adapter_up_factor, cotangent)
    return values, grad_acts, grad_down_t.T, grad_up


def body(acts, w_value, adapt_down, adapter_up_factor, cotangent):
    whole = lax.all_gather(acts, "col", axis=1, tiled=True)
    tok_count = whole.shape[0]
    width = whole.shape[1]
    down_full = lax.all_gather(adapt_down, "row", axis=0, tiled=True)
    piece = lax.all_gather(w_value, "row", axis=0, tiled=True)
    span = whole
    base_output = jnp.dot(span, piece, preferred_element_type=jnp.float32)
    base_output, stored = (base_output, piece)
    low_sum = jnp.dot(whole, down_full, preferred_element_type=jnp.float32)
    low_rank_input = low_sum.astype(jnp.bfloat16)
    values = (
        base_output
        + ADAPTER_SCALE
        * jnp.dot(low_rank_input, adapter_up_factor, preferred_element_type=jnp.float32)
    ).astype(jnp.bfloat16)
    backward_piece = ADAPTER_SCALE * jnp.dot(
        cotangent, adapter_up_factor.T, preferred_element_type=jnp.float32
    )
    backward_result = lax.psum(backward_piece.astype(jnp.bfloat16), "col")
    total_tokens = tok_count * lax.axis_size("row")
    gradient_norm = 1.0 / math.sqrt(total_tokens)
    up_factor_piece = ADAPTER_SCALE * jnp.dot(
        low_rank_input.T, cotangent, preferred_element_type=jnp.float32
    )
    up_factor_gradient = lax.psum(up_factor_piece, "row") * gradient_norm
    col_index = lax.axis_index("col")
    pair_count = lax.axis_size("col")
    tok_half = tok_count // pair_count
    mine_acts = lax.dynamic_slice_in_dim(whole, col_index * tok_half, tok_half, 0)
    mine_back = lax.dynamic_slice_in_dim(backward_result, col_index * tok_half, tok_half, 0)
    span = mine_acts
    grad_down = (
        lax.psum_scatter(
            jnp.dot(span.T, mine_back, preferred_element_type=jnp.float32),
            ("row", "col"),
            scatter_dimension=0,
            tiled=True,
        )
        * gradient_norm
    )
    d_half = width // pair_count
    down_mine = lax.dynamic_slice_in_dim(down_full, col_index * d_half, d_half, 0)
    adapter_dx = jnp.dot(backward_result, down_mine.T, preferred_element_type=jnp.float32)
    partial_dx = jnp.dot(cotangent, stored.T, preferred_element_type=jnp.float32)
    base_dx = lax.psum_scatter(
        partial_dx.astype(jnp.bfloat16), "col", scatter_dimension=1, tiled=True
    ).astype(jnp.float32)
    grad_acts = (base_dx + adapter_dx).astype(jnp.bfloat16)
    return (values, grad_acts, grad_down, up_factor_gradient)


def pick(mesh, *arrays):
    rows, tiles = lax.axis_size("row"), arrays[1].shape[0] % (256 * PIECES) == 0
    fits = rows % 4 == 0 and mesh.shape["groups"] == 2 and mesh.shape["col"] == 2
    step = kernel_body if fits and tiles else body
    return step(*arrays)


def solution(mesh):
    return jax.shard_map(
        functools.partial(pick, mesh),
        mesh=mesh,
        in_specs=(
            P(("groups", "row"), "col"),
            P("row", "col"),
            P("row", None),
            P(None, "col"),
            P(("groups", "row"), "col"),
        ),
        out_specs=(
            P(("groups", "row"), "col"),
            P(("groups", "row"), "col"),
            P(("groups", "row", "col"), None),
            P("groups", "col"),
        ),
        check_vma=False,
    )
```

```python
import functools
import math

import jax
import jax.numpy as jnp
from jax import lax
from jax.experimental import pallas as pl
from jax.experimental.pallas import tpu as pltpu
from jax.sharding import PartitionSpec as P

ADAPTER_SCALE = 2.0
MESH = pl.DeviceIdType.MESH
PIECES = 4
F32 = jnp.float32
BF16 = jnp.bfloat16


def dot(a, b, da=1, db=0):
    return lax.dot_general(a, b, (((da,), (db,)), ((), ())), preferred_element_type=F32)


def exchange_kernel(
    nz,
    norm,
    acts,
    w,
    down_t,
    up,
    cot,
    values,
    gacts,
    gdown,
    gup,
    xa,
    ct,
    uf,
    df,
    wf,
    gds,
    gdr,
    lows,
    lowr,
    ups,
    upx,
    upz,
    upd,
    gas,
    vs,
    vr,
    vacc,
    s_acts,
    r_acts,
    s_cot,
    r_cot,
    s_up,
    r_up,
    s_dn,
    r_dn,
    s_dh,
    s_df,
    r_df,
    s_w,
    r_w,
    s_wl,
    r_wl,
    s_f,
    r_f,
    s_h,
    s_in,
    s_gd,
    r_gd,
    s_low,
    r_low,
    s_ux,
    r_ux,
    s_uz,
    r_uz,
    s_ud,
    r_ud,
    s_ga,
    r_ga,
    s_v,
    r_v,
):
    y, row, c = lax.axis_index("groups"), lax.axis_index("row"), lax.axis_index("col")
    z, x = row // 2, row % 2
    tok, depth, feat = acts.shape[0], w.shape[0], w.shape[1]
    rank = up.shape[0]
    half, hr = depth // 2, rank // 2
    rows = half // PIECES
    dr = rank // 2
    blocks = nz // 2
    home, place = z // blocks, z % blocks
    xo, co, yo = 1 - x, 1 - c, 1 - y

    def dev(yy, zz, xx, cc):
        return (yy, zz * 2 + xx, cc)

    def cols(i, n):
        return pl.ds(pl.multiple_of(i * n, n), n)

    def rc(src, dst, ss, rs, to):
        return pltpu.make_async_remote_copy(
            src_ref=src, dst_ref=dst, send_sem=ss, recv_sem=rs, device_id=to, device_id_type=MESH
        )

    other = dev(y, z, xo, c)

    def arrived(dst, rs):
        rc(dst, dst, rs, rs, other).wait_recv()

    mates = [(x, co), (xo, c), (xo, co)]
    zs = [lax.rem(z + k, nz) for k in range(1, nz)]

    barrier = pltpu.get_barrier_semaphore()
    peers = [dev(y, z, a, b) for a, b in mates] + [dev(yo, z, x, c)]
    peers += [dev(y, t, x, b) for t in zs for b in range(2)]
    for p in peers:
        pl.semaphore_signal(barrier, inc=1, device_id=p, device_id_type=MESH)
    pl.semaphore_wait(barrier, len(peers))

    sent = []

    mine = (cols(x, tok), cols(c, feat))
    for i, (a, b) in enumerate(mates):
        cp = rc(cot, ct.at[mine], s_cot.at[i], r_cot.at[x * 2 + c], dev(y, z, a, b))
        cp.start()
        sent.append(cp)
    cp = rc(up, uf.at[:, cols(c, feat)], s_up, r_up, dev(y, z, x, co))
    cp.start()
    sent.append(cp)
    for b in range(blocks):
        cp = rc(
            acts.at[:, cols(b * 2 + xo, depth)],
            xa.at[b, cols(x, tok), :],
            s_acts.at[b],
            r_acts.at[b],
            other,
        )
        cp.start()
        sent.append(cp)

    w_local = rc(w, wf.at[place, :, cols(c, feat)], s_wl, r_wl, dev(y, z, x, co))
    steps = [(i, t, (t >= 0) & (t < nz)) for i, t in enumerate((z + 1, z - 1))]
    own_sends = []

    def send_if(used, cp):
        own_sends.append((used, cp))

        @pl.when(used)
        def _():
            cp.start()

    for i, t, there in steps:
        part = cols(y, dr)
        to = dev(y, jnp.clip(t, 0, nz - 1), x, c)
        send_if(
            there & (c == home),
            rc(down_t.at[part, :], df.at[place, part, :], s_dn.at[i], r_dn.at[place], to),
        )
    for q in range(PIECES):
        for i, t, there in steps:
            piece = cols(q * 2 + y, rows)
            to = dev(y, jnp.clip(t, 0, nz - 1), x, home)
            send_if(
                there,
                rc(
                    w.at[piece, :],
                    wf.at[place, piece, cols(c, feat)],
                    s_w.at[i, q],
                    r_w.at[place, c, q],
                    to,
                ),
            )

    @pl.when(c != home)
    def _():
        w_local.start()

    into = [
        pltpu.make_async_copy(cot, ct.at[mine], s_in.at[0]),
        pltpu.make_async_copy(up, uf.at[:, cols(c, feat)], s_in.at[1]),
    ]
    for b in range(blocks):
        into.append(
            pltpu.make_async_copy(
                acts.at[:, cols(b * 2 + x, depth)], xa.at[b, cols(x, tok), :], s_in.at[4 + b]
            )
        )
    into_home = [
        pltpu.make_async_copy(down_t, df.at[place], s_in.at[2]),
        pltpu.make_async_copy(w, wf.at[place, :, cols(c, feat)], s_in.at[3]),
    ]
    for cp in into:
        cp.start()

    @pl.when(c == home)
    def _():
        for cp in into_home:
            cp.start()

    def in_order(i, first):
        return jnp.where(
            c == home, lax.rem(place + first + i, blocks), jnp.where(c > home, i, blocks - 1 - i)
        )

    def pass_piece(b, piece, s_next, s_side, r_here, r_side):
        source = c * blocks + b
        absent = source != z
        t = jnp.where(source < z, z + 1, z - 1)
        more = absent & (t >= 0) & (t < nz)

        @pl.when(absent)
        def _():
            arrived(piece, r_here)

        send_if(more, rc(piece, piece, s_next, r_here, dev(y, jnp.clip(t, 0, nz - 1), x, c)))
        send_if(absent, rc(piece, piece, s_side, r_side, dev(yo, z, x, c)))

    def pass_down(b):
        piece = df.at[b, cols(y, dr), :]
        pass_piece(b, piece, s_dh.at[b], s_df.at[b], r_dn.at[b], r_df.at[b])

    def pass_on(b, q):
        for e in range(2):
            pass_piece(
                b,
                wf.at[b, cols(q * 2 + y, rows), pl.ds(e * feat, feat)],
                s_h.at[b, e, q],
                s_f.at[b, e, q],
                r_w.at[b, e, q],
                r_f.at[b, e, q],
            )

    pass_down(in_order(0, 1))
    for q in range(PIECES):
        pass_on(in_order(0, 1), q)
    for i in range(1, blocks):
        pass_down(in_order(i, 1))

    for cp in into:
        cp.wait()

    @pl.when(c == home)
    def _():
        for cp in into_home:
            cp.wait()

    for a, b in mates:
        arrived(ct.at[cols(a, tok), cols(b, feat)], r_cot.at[a * 2 + b])
    arrived(uf.at[:, cols(co, feat)], r_up)
    back = (ADAPTER_SCALE * dot(ct[...], uf[...], 1, 1)).astype(BF16)
    gd_copies = []
    for b in range(blocks):
        arrived(xa.at[b, cols(xo, tok), :], r_acts.at[b])
        gds[b] = dot(back, xa[b], 0, 0).astype(BF16)
        t = c * blocks + b
        for e in range(2):
            cp = rc(
                gds.at[b, :, pl.ds(e * half, half)],
                gdr.at[z],
                s_gd.at[b, e],
                r_gd.at[z],
                dev(y, t, x, e),
            )
            here = (t == z) & (c == e)
            gd_copies.append((here, b, e, cp))

    low_t = jnp.zeros((rank, 2 * tok), F32)
    for b in range(blocks):

        @pl.when(c * blocks + b != z)
        def _():
            arrived(df.at[b, cols(yo, dr), :], r_df.at[b])

        low_t += dot(df[b], xa[b], 1, 1)
    lows[0] = low_t[:, :tok]
    lows[1] = low_t[:, tok:]
    for i, (a, b) in enumerate(mates):
        cp = rc(lows.at[a], lowr.at[x * 2 + c], s_low.at[i], r_low.at[x * 2 + c], dev(y, z, a, b))
        cp.start()
        sent.append(cp)
    def send_values():
        vs[...] = vacc[...].astype(BF16)
        for i, (a, b) in enumerate(mates):
            cp = rc(
                vs.at[cols(a, tok), cols(b, feat)],
                vr.at[x * 2 + c],
                s_v.at[i],
                r_v.at[x * 2 + c],
                dev(y, z, a, b),
            )
            cp.start()
            sent.append(cp)

    def work_on(i, q):
        b = in_order(i, 0)
        absent = c * blocks + b != z
        chunk = pl.ds(q * 2 * rows, 2 * rows)
        if q == 0:

            @pl.when(jnp.logical_not(absent))
            def _():
                arrived(wf.at[b, :, cols(co, feat)], r_wl)

        @pl.when(absent)
        def _():
            for e in range(2):
                arrived(wf.at[b, cols(q * 2 + yo, rows), pl.ds(e * feat, feat)], r_f.at[b, e, q])

        part = dot(xa[b, :, chunk], wf[b, chunk, :])
        if i == 0 and q == 0:
            vacc[...] = part
        else:
            vacc[...] += part
        if i == blocks - 1 and q == PIECES - 1:
            send_values()
        grad = dot(back, df[b, :, chunk])
        for e in range(2):
            part = dot(
                ct[:, e * feat : (e + 1) * feat], wf[b, chunk, e * feat : (e + 1) * feat], 1, 1
            )
            grad += part.astype(BF16).astype(F32)
        gas[b, :, chunk] = grad.astype(BF16)
        at = cols((b * 2 + x) * PIECES + q, 2 * rows)
        cp = rc(
            gas.at[b, cols(xo, tok), chunk], gacts.at[:, at], s_ga.at[b, q], r_ga.at[b, q], other
        )
        cp.start()
        sent.append(cp)
        gacts[:, at] = gas[b, cols(x, tok), chunk]

    def work_and_pass(i, q):
        work_on(i, q)
        if i + 1 < blocks:
            pass_on(in_order(i + 1, 1), q)

    work_and_pass(0, 0)

    low = lows[x]
    for a, b in mates:
        arrived(lowr.at[a * 2 + b], r_low.at[a * 2 + b])
        low += lowr[a * 2 + b]
    low = low.astype(BF16)

    ups[...] = ADAPTER_SCALE * dot(low, ct[mine])
    cp = rc(ups.at[cols(xo, hr), :], upx, s_ux, r_ux, other)
    cp.start()
    sent.append(cp)
    work_and_pass(0, 1)
    arrived(upx, r_ux)
    upz[z] = (ups[cols(x, hr), :] + upx[...]).astype(BF16)
    for k, t in enumerate(zs):
        cp = rc(upz.at[z], upz.at[z], s_uz.at[k], r_uz.at[z], dev(y, t, x, c))
        cp.start()
        sent.append(cp)

    for n in range(2, blocks * PIECES - 2):
        work_and_pass(n // PIECES, n % PIECES)

    for here, b, e, cp in gd_copies:

        @pl.when(here)
        def _():
            gdr[z] = gds[b, :, e * half : (e + 1) * half]

        @pl.when(jnp.logical_not(here))
        def _():
            cp.start()

    for t in zs:
        arrived(upz.at[t], r_uz.at[t])
    total = upz[0].astype(F32)
    for t in range(1, nz):
        total += upz[t].astype(F32)
    upd[...] = total * norm
    gup[cols(x, hr), :] = upd[...]
    cp = rc(upd, gup.at[cols(x, hr), :], s_ud, r_ud, other)
    cp.start()
    sent.append(cp)

    for n in range(blocks * PIECES - 2, blocks * PIECES):
        work_and_pass(n // PIECES, n % PIECES)

    out = vacc[mine] + ADAPTER_SCALE * dot(low, uf[:, cols(c, feat)], 0, 0)
    for a, b in mates:
        arrived(vr.at[a * 2 + b], r_v.at[a * 2 + b])
        out += vr[a * 2 + b].astype(F32)
    values[...] = out.astype(BF16)

    for t in zs:
        arrived(gdr.at[t], r_gd.at[t])

    @pl.when(c != home)
    def _():
        arrived(gdr.at[z], r_gd.at[z])

    total = gdr[0].astype(F32)
    for t in range(1, nz):
        total += gdr[t].astype(F32)
    gdown[...] = total * norm

    arrived(gup.at[cols(xo, hr), :], r_ud)
    for b in range(blocks):
        for q in range(PIECES):
            at = cols((b * 2 + xo) * PIECES + q, 2 * rows)
            arrived(gacts.at[:, at], r_ga.at[b, q])
    for cp in sent:
        cp.wait_send()
    for here, _, _, cp in gd_copies:

        @pl.when(jnp.logical_not(here))
        def _():
            cp.wait_send()

    for used, cp in own_sends:

        @pl.when(used)
        def _():
            cp.wait_send()

    @pl.when(c != home)
    def _():
        w_local.wait_send()


def kernel_body(acts, w_value, adapt_down, adapter_up_factor, cotangent):
    tok, width = acts.shape
    depth, feat = w_value.shape
    rank = adapter_up_factor.shape[0]
    rows = lax.axis_size("row")
    nz = rows // 2
    blocks, half, hr = nz // 2, depth // 2, rank // 2
    norm = 1.0 / math.sqrt(tok * rows)
    vmem = pl.BlockSpec(memory_space=pltpu.VMEM)
    dma = lambda *s: pltpu.SemaphoreType.DMA(s) if s else pltpu.SemaphoreType.DMA
    scratch = [
        pltpu.VMEM((blocks, 2 * tok, depth), BF16),
        pltpu.VMEM((2 * tok, 2 * feat), BF16),
        pltpu.VMEM((rank, 2 * feat), BF16),
        pltpu.VMEM((blocks, rank, depth), BF16),
        pltpu.VMEM((blocks, depth, 2 * feat), BF16),
        pltpu.VMEM((blocks, rank, depth), BF16),
        pltpu.VMEM((nz, rank, half), BF16),
        pltpu.VMEM((2, rank, tok), F32),
        pltpu.VMEM((4, rank, tok), F32),
        pltpu.VMEM((rank, feat), F32),
        pltpu.VMEM((hr, feat), F32),
        pltpu.VMEM((nz, hr, feat), BF16),
        pltpu.VMEM((hr, feat), F32),
        pltpu.VMEM((blocks, 2 * tok, depth), BF16),
        pltpu.VMEM((2 * tok, 2 * feat), BF16),
        pltpu.VMEM((4, tok, feat), BF16),
        pltpu.VMEM((2 * tok, 2 * feat), F32),
        dma(blocks), dma(blocks),
        dma(3), dma(4),
        dma(), dma(),
        dma(2), dma(blocks), dma(blocks), dma(blocks), dma(blocks),
        dma(2, PIECES), dma(blocks, 2, PIECES),
        dma(), dma(),
        dma(blocks, 2, PIECES), dma(blocks, 2, PIECES),
        dma(blocks, 2, PIECES), dma(4 + blocks),
        dma(blocks, 2), dma(nz),
        dma(3), dma(4),
        dma(), dma(),
        dma(nz - 1), dma(nz),
        dma(), dma(),
        dma(blocks, PIECES), dma(blocks, PIECES),
        dma(3), dma(4),
    ]
    values, grad_acts, grad_down_t, grad_up = pl.pallas_call(
        functools.partial(exchange_kernel, nz, norm),
        out_shape=(
            jax.ShapeDtypeStruct((tok, feat), BF16),
            jax.ShapeDtypeStruct((tok, width), BF16),
            jax.ShapeDtypeStruct((rank, half), F32),
            jax.ShapeDtypeStruct((rank, feat), F32),
        ),
        in_specs=[pl.BlockSpec(memory_space=pltpu.HBM)] * 5,
        out_specs=(vmem,) * 4,
        scratch_shapes=scratch,
        compiler_params=pltpu.CompilerParams(
            collective_id=0, has_side_effects=True, vmem_limit_bytes=62 * 2**20
        ),
    )(acts, w_value, adapt_down.T, adapter_up_factor, cotangent)
    return values, grad_acts, grad_down_t.T, grad_up


def body(acts, w_value, adapt_down, adapter_up_factor, cotangent):
    whole = lax.all_gather(acts, "col", axis=1, tiled=True)
    tok_count = whole.shape[0]
    width = whole.shape[1]
    down_full = lax.all_gather(adapt_down, "row", axis=0, tiled=True)
    piece = lax.all_gather(w_value, "row", axis=0, tiled=True)
    span = whole
    base_output = jnp.dot(span, piece, preferred_element_type=jnp.float32)
    base_output, stored = (base_output, piece)
    low_sum = jnp.dot(whole, down_full, preferred_element_type=jnp.float32)
    low_rank_input = low_sum.astype(jnp.bfloat16)
    values = (
        base_output
        + ADAPTER_SCALE
        * jnp.dot(low_rank_input, adapter_up_factor, preferred_element_type=jnp.float32)
    ).astype(jnp.bfloat16)
    backward_piece = ADAPTER_SCALE * jnp.dot(
        cotangent, adapter_up_factor.T, preferred_element_type=jnp.float32
    )
    backward_result = lax.psum(backward_piece.astype(jnp.bfloat16), "col")
    total_tokens = tok_count * lax.axis_size("row")
    gradient_norm = 1.0 / math.sqrt(total_tokens)
    up_factor_piece = ADAPTER_SCALE * jnp.dot(
        low_rank_input.T, cotangent, preferred_element_type=jnp.float32
    )
    up_factor_gradient = lax.psum(up_factor_piece, "row") * gradient_norm
    col_index = lax.axis_index("col")
    pair_count = lax.axis_size("col")
    tok_half = tok_count // pair_count
    mine_acts = lax.dynamic_slice_in_dim(whole, col_index * tok_half, tok_half, 0)
    mine_back = lax.dynamic_slice_in_dim(backward_result, col_index * tok_half, tok_half, 0)
    span = mine_acts
    grad_down = (
        lax.psum_scatter(
            jnp.dot(span.T, mine_back, preferred_element_type=jnp.float32),
            ("row", "col"),
            scatter_dimension=0,
            tiled=True,
        )
        * gradient_norm
    )
    d_half = width // pair_count
    down_mine = lax.dynamic_slice_in_dim(down_full, col_index * d_half, d_half, 0)
    adapter_dx = jnp.dot(backward_result, down_mine.T, preferred_element_type=jnp.float32)
    partial_dx = jnp.dot(cotangent, stored.T, preferred_element_type=jnp.float32)
    base_dx = lax.psum_scatter(
        partial_dx.astype(jnp.bfloat16), "col", scatter_dimension=1, tiled=True
    ).astype(jnp.float32)
    grad_acts = (base_dx + adapter_dx).astype(jnp.bfloat16)
    return (values, grad_acts, grad_down, up_factor_gradient)


def pick(mesh, *arrays):
    rows, tiles = lax.axis_size("row"), arrays[1].shape[0] % (256 * PIECES) == 0
    fits = rows % 4 == 0 and mesh.shape["groups"] == 2 and mesh.shape["col"] == 2
    step = kernel_body if fits and tiles else body
    return step(*arrays)


def solution(mesh):
    return jax.shard_map(
        functools.partial(pick, mesh),
        mesh=mesh,
        in_specs=(
            P(("groups", "row"), "col"),
            P("row", "col"),
            P("row", None),
            P(None, "col"),
            P(("groups", "row"), "col"),
        ),
        out_specs=(
            P(("groups", "row"), "col"),
            P(("groups", "row"), "col"),
            P(("groups", "row", "col"), None),
            P("groups", "col"),
        ),
        check_vma=False,
    )
```

```python
import functools
import math

import jax
import jax.numpy as jnp
from jax import lax
from jax.experimental import pallas as pl
from jax.experimental.pallas import tpu as pltpu
from jax.sharding import PartitionSpec as P

ADAPTER_SCALE = 2.0
MESH = pl.DeviceIdType.MESH
PIECES = 4
F32 = jnp.float32
BF16 = jnp.bfloat16


def dot(a, b, da=1, db=0):
    return lax.dot_general(a, b, (((da,), (db,)), ((), ())), preferred_element_type=F32)


def exchange_kernel(
    nz,
    norm,
    acts,
    w,
    down_t,
    up,
    cot,
    values,
    gacts,
    gdown,
    gup,
    xa,
    ct,
    uf,
    df,
    wf,
    gds,
    gdr,
    lows,
    lowr,
    ups,
    upx,
    upz,
    upd,
    gas,
    vs,
    vr,
    vacc,
    s_acts,
    r_acts,
    s_cot,
    r_cot,
    s_up,
    r_up,
    s_dn,
    r_dn,
    s_dh,
    s_df,
    r_df,
    s_w,
    r_w,
    s_wl,
    r_wl,
    s_f,
    r_f,
    s_h,
    s_in,
    s_gd,
    r_gd,
    s_low,
    r_low,
    s_ux,
    r_ux,
    s_uz,
    r_uz,
    s_ud,
    r_ud,
    s_ga,
    r_ga,
    s_v,
    r_v,
):
    y, row, c = lax.axis_index("groups"), lax.axis_index("row"), lax.axis_index("col")
    z, x = row // 2, row % 2
    tok, depth, feat = acts.shape[0], w.shape[0], w.shape[1]
    rank = up.shape[0]
    half, hr = depth // 2, rank // 2
    rows = half // PIECES
    dr = rank // 2
    blocks = nz // 2
    home, place = z // blocks, z % blocks
    xo, co, yo = 1 - x, 1 - c, 1 - y

    def dev(yy, zz, xx, cc):
        return (yy, zz * 2 + xx, cc)

    def cols(i, n):
        return pl.ds(pl.multiple_of(i * n, n), n)

    def rc(src, dst, ss, rs, to):
        return pltpu.make_async_remote_copy(
            src_ref=src, dst_ref=dst, send_sem=ss, recv_sem=rs, device_id=to, device_id_type=MESH
        )

    other = dev(y, z, xo, c)

    def arrived(dst, rs):
        rc(dst, dst, rs, rs, other).wait_recv()

    mates = [(x, co), (xo, c), (xo, co)]
    zs = [lax.rem(z + k, nz) for k in range(1, nz)]

    barrier = pltpu.get_barrier_semaphore()
    peers = [dev(y, z, a, b) for a, b in mates] + [dev(yo, z, x, c)]
    peers += [dev(y, t, x, b) for t in zs for b in range(2)]
    for p in peers:
        pl.semaphore_signal(barrier, inc=1, device_id=p, device_id_type=MESH)
    pl.semaphore_wait(barrier, len(peers))

    sent = []

    mine = (cols(x, tok), cols(c, feat))
    for i, (a, b) in enumerate(mates):
        cp = rc(cot, ct.at[mine], s_cot.at[i], r_cot.at[x * 2 + c], dev(y, z, a, b))
        cp.start()
        sent.append(cp)
    cp = rc(up, uf.at[:, cols(c, feat)], s_up, r_up, dev(y, z, x, co))
    cp.start()
    sent.append(cp)
    for b in range(blocks):
        cp = rc(
            acts.at[:, cols(b * 2 + xo, depth)],
            xa.at[b, cols(x, tok), :],
            s_acts.at[b],
            r_acts.at[b],
            other,
        )
        cp.start()
        sent.append(cp)

    w_local = rc(w, wf.at[place, :, cols(c, feat)], s_wl, r_wl, dev(y, z, x, co))
    steps = [(i, t, (t >= 0) & (t < nz)) for i, t in enumerate((z + 1, z - 1))]
    own_sends = []

    def send_if(used, cp):
        own_sends.append((used, cp))

        @pl.when(used)
        def _():
            cp.start()

    for i, t, there in steps:
        part = cols(y, dr)
        to = dev(y, jnp.clip(t, 0, nz - 1), x, c)
        send_if(
            there & (c == home),
            rc(down_t.at[part, :], df.at[place, part, :], s_dn.at[i], r_dn.at[place], to),
        )
    for q in range(PIECES):
        for i, t, there in steps:
            piece = cols(q * 2 + y, rows)
            to = dev(y, jnp.clip(t, 0, nz - 1), x, home)
            send_if(
                there,
                rc(
                    w.at[piece, :],
                    wf.at[place, piece, cols(c, feat)],
                    s_w.at[i, q],
                    r_w.at[place, c, q],
                    to,
                ),
            )

    @pl.when(c != home)
    def _():
        w_local.start()

    into = [
        pltpu.make_async_copy(cot, ct.at[mine], s_in.at[0]),
        pltpu.make_async_copy(up, uf.at[:, cols(c, feat)], s_in.at[1]),
    ]
    for b in range(blocks):
        into.append(
            pltpu.make_async_copy(
                acts.at[:, cols(b * 2 + x, depth)], xa.at[b, cols(x, tok), :], s_in.at[4 + b]
            )
        )
    into_home = [
        pltpu.make_async_copy(down_t, df.at[place], s_in.at[2]),
        pltpu.make_async_copy(w, wf.at[place, :, cols(c, feat)], s_in.at[3]),
    ]
    for cp in into:
        cp.start()

    @pl.when(c == home)
    def _():
        for cp in into_home:
            cp.start()

    def in_order(i, first):
        return jnp.where(
            c == home, lax.rem(place + first + i, blocks), jnp.where(c > home, i, blocks - 1 - i)
        )

    def pass_piece(b, piece, s_next, s_side, r_here, r_side):
        source = c * blocks + b
        absent = source != z
        t = jnp.where(source < z, z + 1, z - 1)
        more = absent & (t >= 0) & (t < nz)

        @pl.when(absent)
        def _():
            arrived(piece, r_here)

        send_if(more, rc(piece, piece, s_next, r_here, dev(y, jnp.clip(t, 0, nz - 1), x, c)))
        send_if(absent, rc(piece, piece, s_side, r_side, dev(yo, z, x, c)))

    def pass_down(b):
        piece = df.at[b, cols(y, dr), :]
        pass_piece(b, piece, s_dh.at[b], s_df.at[b], r_dn.at[b], r_df.at[b])

    def pass_on(b, q):
        for e in range(2):
            pass_piece(
                b,
                wf.at[b, cols(q * 2 + y, rows), pl.ds(e * feat, feat)],
                s_h.at[b, e, q],
                s_f.at[b, e, q],
                r_w.at[b, e, q],
                r_f.at[b, e, q],
            )

    pass_down(in_order(0, 1))
    for q in range(PIECES):
        pass_on(in_order(0, 1), q)
    for i in range(1, blocks):
        pass_down(in_order(i, 1))

    for cp in into:
        cp.wait()

    @pl.when(c == home)
    def _():
        for cp in into_home:
            cp.wait()

    for a, b in mates:
        arrived(ct.at[cols(a, tok), cols(b, feat)], r_cot.at[a * 2 + b])
    arrived(uf.at[:, cols(co, feat)], r_up)
    back = (ADAPTER_SCALE * dot(ct[...], uf[...], 1, 1)).astype(BF16)
    gd_copies = []
    for b in range(blocks):
        arrived(xa.at[b, cols(xo, tok), :], r_acts.at[b])
        gds[b] = dot(back, xa[b], 0, 0).astype(BF16)
        t = c * blocks + b
        for e in range(2):
            cp = rc(
                gds.at[b, :, pl.ds(e * half, half)],
                gdr.at[z],
                s_gd.at[b, e],
                r_gd.at[z],
                dev(y, t, x, e),
            )
            here = (t == z) & (c == e)
            gd_copies.append((here, b, e, cp))

    low_t = jnp.zeros((rank, 2 * tok), F32)
    for b in range(blocks):

        @pl.when(c * blocks + b != z)
        def _():
            arrived(df.at[b, cols(yo, dr), :], r_df.at[b])

        low_t += dot(df[b], xa[b], 1, 1)
    lows[0] = low_t[:, :tok]
    lows[1] = low_t[:, tok:]
    for i, (a, b) in enumerate(mates):
        cp = rc(lows.at[a], lowr.at[x * 2 + c], s_low.at[i], r_low.at[x * 2 + c], dev(y, z, a, b))
        cp.start()
        sent.append(cp)
    def send_values():
        vs[...] = vacc[...].astype(BF16)
        for i, (a, b) in enumerate(mates):
            cp = rc(
                vs.at[cols(a, tok), cols(b, feat)],
                vr.at[x * 2 + c],
                s_v.at[i],
                r_v.at[x * 2 + c],
                dev(y, z, a, b),
            )
            cp.start()
            sent.append(cp)

    def work_on(i, q):
        b = in_order(i, 0)
        absent = c * blocks + b != z
        chunk = pl.ds(q * 2 * rows, 2 * rows)
        if q == 0:

            @pl.when(jnp.logical_not(absent))
            def _():
                arrived(wf.at[b, :, cols(co, feat)], r_wl)

        @pl.when(absent)
        def _():
            for e in range(2):
                arrived(wf.at[b, cols(q * 2 + yo, rows), pl.ds(e * feat, feat)], r_f.at[b, e, q])

        part = dot(xa[b, :, chunk], wf[b, chunk, :])
        if i == 0 and q == 0:
            vacc[...] = part
        else:
            vacc[...] += part
        if i == blocks - 1 and q == PIECES - 1:
            send_values()
        grad = dot(back, df[b, :, chunk])
        for e in range(2):
            part = dot(
                ct[:, e * feat : (e + 1) * feat], wf[b, chunk, e * feat : (e + 1) * feat], 1, 1
            )
            grad += part.astype(BF16).astype(F32)
        gas[b, :, chunk] = grad.astype(BF16)
        at = cols((b * 2 + x) * PIECES + q, 2 * rows)
        cp = rc(
            gas.at[b, cols(xo, tok), chunk], gacts.at[:, at], s_ga.at[b, q], r_ga.at[b, q], other
        )
        cp.start()
        sent.append(cp)
        gacts[:, at] = gas[b, cols(x, tok), chunk]

    def work_and_pass(i, q):
        if i + 1 < blocks:
            pass_on(in_order(i + 1, 1), q)
        work_on(i, q)

    work_and_pass(0, 0)

    low = lows[x]
    for a, b in mates:
        arrived(lowr.at[a * 2 + b], r_low.at[a * 2 + b])
        low += lowr[a * 2 + b]
    low = low.astype(BF16)

    ups[...] = ADAPTER_SCALE * dot(low, ct[mine])
    cp = rc(ups.at[cols(xo, hr), :], upx, s_ux, r_ux, other)
    cp.start()
    sent.append(cp)
    work_and_pass(0, 1)
    arrived(upx, r_ux)
    upz[z] = (ups[cols(x, hr), :] + upx[...]).astype(BF16)
    for k, t in enumerate(zs):
        cp = rc(upz.at[z], upz.at[z], s_uz.at[k], r_uz.at[z], dev(y, t, x, c))
        cp.start()
        sent.append(cp)

    for n in range(2, blocks * PIECES - 2):
        work_and_pass(n // PIECES, n % PIECES)

    for here, b, e, cp in gd_copies:

        @pl.when(here)
        def _():
            gdr[z] = gds[b, :, e * half : (e + 1) * half]

        @pl.when(jnp.logical_not(here))
        def _():
            cp.start()

    for t in zs:
        arrived(upz.at[t], r_uz.at[t])
    total = upz[0].astype(F32)
    for t in range(1, nz):
        total += upz[t].astype(F32)
    upd[...] = total * norm
    gup[cols(x, hr), :] = upd[...]
    cp = rc(upd, gup.at[cols(x, hr), :], s_ud, r_ud, other)
    cp.start()
    sent.append(cp)

    for n in range(blocks * PIECES - 2, blocks * PIECES):
        work_and_pass(n // PIECES, n % PIECES)

    out = vacc[mine] + ADAPTER_SCALE * dot(low, uf[:, cols(c, feat)], 0, 0)
    for a, b in mates:
        arrived(vr.at[a * 2 + b], r_v.at[a * 2 + b])
        out += vr[a * 2 + b].astype(F32)
    values[...] = out.astype(BF16)

    for t in zs:
        arrived(gdr.at[t], r_gd.at[t])

    @pl.when(c != home)
    def _():
        arrived(gdr.at[z], r_gd.at[z])

    total = gdr[0].astype(F32)
    for t in range(1, nz):
        total += gdr[t].astype(F32)
    gdown[...] = total * norm

    arrived(gup.at[cols(xo, hr), :], r_ud)
    for b in range(blocks):
        for q in range(PIECES):
            at = cols((b * 2 + xo) * PIECES + q, 2 * rows)
            arrived(gacts.at[:, at], r_ga.at[b, q])
    for cp in sent:
        cp.wait_send()
    for here, _, _, cp in gd_copies:

        @pl.when(jnp.logical_not(here))
        def _():
            cp.wait_send()

    for used, cp in own_sends:

        @pl.when(used)
        def _():
            cp.wait_send()

    @pl.when(c != home)
    def _():
        w_local.wait_send()


def kernel_body(acts, w_value, adapt_down, adapter_up_factor, cotangent):
    tok, width = acts.shape
    depth, feat = w_value.shape
    rank = adapter_up_factor.shape[0]
    rows = lax.axis_size("row")
    nz = rows // 2
    blocks, half, hr = nz // 2, depth // 2, rank // 2
    norm = 1.0 / math.sqrt(tok * rows)
    vmem = pl.BlockSpec(memory_space=pltpu.VMEM)
    dma = lambda *s: pltpu.SemaphoreType.DMA(s) if s else pltpu.SemaphoreType.DMA
    scratch = [
        pltpu.VMEM((blocks, 2 * tok, depth), BF16),
        pltpu.VMEM((2 * tok, 2 * feat), BF16),
        pltpu.VMEM((rank, 2 * feat), BF16),
        pltpu.VMEM((blocks, rank, depth), BF16),
        pltpu.VMEM((blocks, depth, 2 * feat), BF16),
        pltpu.VMEM((blocks, rank, depth), BF16),
        pltpu.VMEM((nz, rank, half), BF16),
        pltpu.VMEM((2, rank, tok), F32),
        pltpu.VMEM((4, rank, tok), F32),
        pltpu.VMEM((rank, feat), F32),
        pltpu.VMEM((hr, feat), F32),
        pltpu.VMEM((nz, hr, feat), BF16),
        pltpu.VMEM((hr, feat), F32),
        pltpu.VMEM((blocks, 2 * tok, depth), BF16),
        pltpu.VMEM((2 * tok, 2 * feat), BF16),
        pltpu.VMEM((4, tok, feat), BF16),
        pltpu.VMEM((2 * tok, 2 * feat), F32),
        dma(blocks), dma(blocks),
        dma(3), dma(4),
        dma(), dma(),
        dma(2), dma(blocks), dma(blocks), dma(blocks), dma(blocks),
        dma(2, PIECES), dma(blocks, 2, PIECES),
        dma(), dma(),
        dma(blocks, 2, PIECES), dma(blocks, 2, PIECES),
        dma(blocks, 2, PIECES), dma(4 + blocks),
        dma(blocks, 2), dma(nz),
        dma(3), dma(4),
        dma(), dma(),
        dma(nz - 1), dma(nz),
        dma(), dma(),
        dma(blocks, PIECES), dma(blocks, PIECES),
        dma(3), dma(4),
    ]
    values, grad_acts, grad_down_t, grad_up = pl.pallas_call(
        functools.partial(exchange_kernel, nz, norm),
        out_shape=(
            jax.ShapeDtypeStruct((tok, feat), BF16),
            jax.ShapeDtypeStruct((tok, width), BF16),
            jax.ShapeDtypeStruct((rank, half), F32),
            jax.ShapeDtypeStruct((rank, feat), F32),
        ),
        in_specs=[pl.BlockSpec(memory_space=pltpu.HBM)] * 5,
        out_specs=(vmem,) * 4,
        scratch_shapes=scratch,
        compiler_params=pltpu.CompilerParams(
            collective_id=0, has_side_effects=True, vmem_limit_bytes=62 * 2**20
        ),
    )(acts, w_value, adapt_down.T, adapter_up_factor, cotangent)
    return values, grad_acts, grad_down_t.T, grad_up


def body(acts, w_value, adapt_down, adapter_up_factor, cotangent):
    whole = lax.all_gather(acts, "col", axis=1, tiled=True)
    tok_count = whole.shape[0]
    width = whole.shape[1]
    down_full = lax.all_gather(adapt_down, "row", axis=0, tiled=True)
    piece = lax.all_gather(w_value, "row", axis=0, tiled=True)
    span = whole
    base_output = jnp.dot(span, piece, preferred_element_type=jnp.float32)
    base_output, stored = (base_output, piece)
    low_sum = jnp.dot(whole, down_full, preferred_element_type=jnp.float32)
    low_rank_input = low_sum.astype(jnp.bfloat16)
    values = (
        base_output
        + ADAPTER_SCALE
        * jnp.dot(low_rank_input, adapter_up_factor, preferred_element_type=jnp.float32)
    ).astype(jnp.bfloat16)
    backward_piece = ADAPTER_SCALE * jnp.dot(
        cotangent, adapter_up_factor.T, preferred_element_type=jnp.float32
    )
    backward_result = lax.psum(backward_piece.astype(jnp.bfloat16), "col")
    total_tokens = tok_count * lax.axis_size("row")
    gradient_norm = 1.0 / math.sqrt(total_tokens)
    up_factor_piece = ADAPTER_SCALE * jnp.dot(
        low_rank_input.T, cotangent, preferred_element_type=jnp.float32
    )
    up_factor_gradient = lax.psum(up_factor_piece, "row") * gradient_norm
    col_index = lax.axis_index("col")
    pair_count = lax.axis_size("col")
    tok_half = tok_count // pair_count
    mine_acts = lax.dynamic_slice_in_dim(whole, col_index * tok_half, tok_half, 0)
    mine_back = lax.dynamic_slice_in_dim(backward_result, col_index * tok_half, tok_half, 0)
    span = mine_acts
    grad_down = (
        lax.psum_scatter(
            jnp.dot(span.T, mine_back, preferred_element_type=jnp.float32),
            ("row", "col"),
            scatter_dimension=0,
            tiled=True,
        )
        * gradient_norm
    )
    d_half = width // pair_count
    down_mine = lax.dynamic_slice_in_dim(down_full, col_index * d_half, d_half, 0)
    adapter_dx = jnp.dot(backward_result, down_mine.T, preferred_element_type=jnp.float32)
    partial_dx = jnp.dot(cotangent, stored.T, preferred_element_type=jnp.float32)
    base_dx = lax.psum_scatter(
        partial_dx.astype(jnp.bfloat16), "col", scatter_dimension=1, tiled=True
    ).astype(jnp.float32)
    grad_acts = (base_dx + adapter_dx).astype(jnp.bfloat16)
    return (values, grad_acts, grad_down, up_factor_gradient)


def pick(mesh, *arrays):
    rows, tiles = lax.axis_size("row"), arrays[1].shape[0] % (256 * PIECES) == 0
    fits = rows % 4 == 0 and mesh.shape["groups"] == 2 and mesh.shape["col"] == 2
    step = kernel_body if fits and tiles else body
    return step(*arrays)


def solution(mesh):
    return jax.shard_map(
        functools.partial(pick, mesh),
        mesh=mesh,
        in_specs=(
            P(("groups", "row"), "col"),
            P("row", "col"),
            P("row", None),
            P(None, "col"),
            P(("groups", "row"), "col"),
        ),
        out_specs=(
            P(("groups", "row"), "col"),
            P(("groups", "row"), "col"),
            P(("groups", "row", "col"), None),
            P("groups", "col"),
        ),
        check_vma=False,
    )
```
